32 devices in a mesh: grid: 8 (over y, x, core), band: 4 (over z).
Axes of the slice: x: 2, y: 2, z: 4, core: 2. Of those that a mesh axis runs over, the one named last changes fastest.
Arguments:
- orbitals: bfloat16 [8192, 512], P('grid', 'band'), may hold values from -6 to 6
- rotation: bfloat16 [512, 32768], P('grid', 'band'), may hold values from -0.25 to 0.25
Outputs:
- rotated: bfloat16 [8192, 32768], P('grid', 'band')
The draws below stay inside these ranges and needn't reach their ends.
All inputs are finite; a program needn't handle non-finite values.
Results may differ from the reference program's by a relative error of at most 0.001.
Values may be sent and summed in bfloat16 or wider, within the bound.
A program may use at most 64 MiB of HBM per device.

```python
import jax
import jax.numpy as jnp

NB = 32768
KIN = 512
POINTS = 8192


def levels(stream_key, shape, pieces, low, largest):
    level = 1.0
    for position, shards_of in pieces:
        steps = jax.random.uniform(jax.random.fold_in(jax.random.fold_in(stream_key, 6), position), (shards_of,), jnp.float32, low / len(pieces), largest / len(pieces))
        level = level * jnp.repeat(jnp.exp(steps), shape[position] // shards_of).reshape((-1,) + (1,) * (len(shape) - 1 - position))
    return level


def scatter_about(rng, shape, deviation, reach, shards=(), held_as=jnp.bfloat16):
    result = deviation * jax.random.normal(rng, shape, jnp.float32)
    if shards:
        result = result * levels(rng, shape, shards, -0.22, 0.18)
    return jnp.clip(result, -reach, reach).astype(held_as)


def setup_inputs(seed: int = 0) -> dict:
    streams_of = jax.random.split(jax.random.key(seed), 3)
    return {
        "orbitals": scatter_about(streams_of[0], (POINTS, KIN), 1.0, 6.0, ((0, 8), (1, 4))),
        "rotation": scatter_about(streams_of[1], (KIN, NB), KIN ** -0.5, 0.25, ((0, 8), (1, 4))),
    }


def reference(orbitals, rotation):
    product = jnp.dot(orbitals, rotation, preferred_element_type=jnp.float32)
    return product.astype(jnp.bfloat16)
```

```python
import functools

import jax
import jax.numpy as jnp
from jax import lax
from jax.experimental import pallas as pl
from jax.experimental.pallas import tpu as pltpu
from jax.sharding import PartitionSpec as P

CHUNKS = 16
EARLY = 4
AHEAD = 3


def gather_multiply(
    orb_ref, rot_ref, out_ref, gathered, points,
    early_send, early_recv, late_send, late_recv, pass_send, pass_recv,
    pair_send, pair_recv, line_send, line_recv, local_sem,
):
    depth, columns = rot_ref.shape
    inner = orb_ref.shape[1]
    half = depth // 2
    wide, narrow = columns // EARLY, columns // CHUNKS

    me = lax.axis_index("grid")
    z = lax.axis_index("band")
    nz = lax.axis_size("band")
    chip, core = me // 2, me % 2
    y, x = chip // 2, chip % 2
    chip_x = y * 2 + (1 - x)
    chip_y = (1 - y) * 2 + x
    chip_far = (1 - y) * 2 + (1 - x)
    sides = (chip_x, chip_y)

    def device(a_chip, a_core=core, a_z=z):
        return {"grid": a_chip * 2 + a_core, "band": a_z}

    first = (slice(0, half), slice(half, depth))

    def cols(j, width):
        return pl.ds(pl.multiple_of(j * width, width), width)

    def remote(src, dst, send, recv, to):
        return pltpu.make_async_remote_copy(
            src_ref=src, dst_ref=dst, send_sem=send, recv_sem=recv, device_id=to,
            device_id_type=pl.DeviceIdType.MESH,
        )

    def early(d, p):
        where = cols(p, wide)
        return remote(
            rot_ref.at[first[d], where], gathered.at[chip, core, first[d], where],
            early_send.at[d, p], early_recv.at[d, p], device(sides[d]))

    def late(d, j):
        where = cols(j, narrow)
        return remote(
            rot_ref.at[first[1 - d], where], gathered.at[chip, core, first[1 - d], where],
            late_send.at[d, j], late_recv.at[d, j], device(sides[d]))

    def passed(d, j):
        where = cols(j, narrow)
        ref = gathered.at[sides[1 - d], core, first[1 - d], where]
        return remote(ref, ref, pass_send.at[d, j], pass_recv.at[d, j], device(sides[d]))

    def pair(j):
        ref = gathered.at[:, core, :, cols(j, narrow)]
        return remote(ref, ref, pair_send.at[j], pair_recv.at[j], device(chip, 1 - core))

    def line(up, k):
        origin = z - k if up else z + k
        to = z + 1 if up else z - 1
        dst = points.at[:, pl.ds(pl.multiple_of(origin * inner, inner), inner)]
        d = 0 if up else 1
        return remote(
            orb_ref if k == 0 else dst, dst,
            line_send.at[d, k], line_recv.at[d, k], device(chip, core, to))

    def line_has(up, k):
        return (z >= k) & (z < nz - 1) if up else (z <= nz - 1 - k) & (z > 0)

    def line_gets(up, k):
        return z >= k + 1 if up else z <= nz - 2 - k

    def line_step(k):
        for up in (True, False):
            if k > 0:
                @pl.when(line_gets(up, k - 1))
                def _():
                    line(up, k - 1).wait_recv()
            if k < 3:
                @pl.when(line_has(up, k))
                def _():
                    line(up, k).start()

    barrier = pltpu.get_barrier_semaphore()

    def greet(to):
        pl.semaphore_signal(barrier, inc=1, device_id=to, device_id_type=pl.DeviceIdType.MESH)

    own_rot = pltpu.make_async_copy(rot_ref, gathered.at[chip, core], local_sem.at[0])
    own_orb = pltpu.make_async_copy(
        orb_ref, points.at[:, pl.ds(pl.multiple_of(z * inner, inner), inner)], local_sem.at[1])
    own_rot.start()
    own_orb.start()

    for to in (device(chip_x), device(chip_y), device(chip, 1 - core)):
        greet(to)

    @pl.when(z > 0)
    def _():
        greet(device(chip, core, z - 1))

    @pl.when(z < nz - 1)
    def _():
        greet(device(chip, core, z + 1))

    middle = (z > 0) & (z < nz - 1)

    @pl.when(middle)
    def _():
        pl.semaphore_wait(barrier, 5)

    @pl.when(jnp.logical_not(middle))
    def _():
        pl.semaphore_wait(barrier, 4)

    def start_early(p):
        for d in (0, 1):
            early(d, p).start()

    def got_early(p):
        for d in (0, 1):
            early(d, p).wait_recv()

    def start_late(j):
        for d in (0, 1):
            late(d, j).start()
            passed(d, j).start()

    def exchange(j):
        for d in (0, 1):
            late(d, j).wait_recv()
            passed(d, j).wait_recv()
        pair(j).start()

    def multiply(j):
        pair(j).wait_recv()
        where = cols(j, narrow)
        block = gathered[:, :, :, where].reshape(8 * depth, narrow)
        out_ref[:, where] = jnp.dot(
            points[...], block, preferred_element_type=jnp.float32
        ).astype(out_ref.dtype)

    line_step(0)
    start_early(0)
    start_early(1)
    got_early(0)
    start_early(2)
    got_early(1)
    line_step(1)
    start_early(3)
    own_rot.wait()
    own_orb.wait()
    got_early(2)
    start_late(0)
    start_late(1)
    got_early(3)
    line_step(2)
    start_late(2)

    def receive(j, _):
        exchange(j)
        start_late(j + AHEAD)
        return 0

    lax.fori_loop(0, 4, receive, 0)
    line_step(3)

    def catch_up(j, _):
        receive(j, 0)

        def one(i, _):
            multiply(i)
            return 0

        lax.fori_loop(2 * (j - 4), 2 * (j - 4) + 2, one, 0)
        return 0

    lax.fori_loop(4, 8, catch_up, 0)

    def steady(j, _):
        exchange(j)

        @pl.when(j + AHEAD < CHUNKS)
        def _():
            start_late(j + AHEAD)

        multiply(j - 1)
        return 0

    exchange(8)
    start_late(8 + AHEAD)
    lax.fori_loop(9, CHUNKS, steady, 0)
    multiply(CHUNKS - 1)

    for p in range(EARLY):
        for d in (0, 1):
            early(d, p).wait_send()

    def sent(j, _):
        for d in (0, 1):
            late(d, j).wait_send()
            passed(d, j).wait_send()
        pair(j).wait_send()
        return 0

    lax.fori_loop(0, CHUNKS, sent, 0)
    for k in range(3):
        for up in (True, False):
            @pl.when(line_has(up, k))
            def _():
                line(up, k).wait_send()


def in_kernel(orbitals, rotation):
    points, inner = orbitals.shape
    depth, columns = rotation.shape
    dma = pltpu.SemaphoreType.DMA
    return pl.pallas_call(
        gather_multiply,
        out_shape=pltpu.VMEM((points, columns), jnp.bfloat16),
        in_specs=[pl.BlockSpec(memory_space=pl.ANY)] * 2,
        out_specs=pl.BlockSpec(memory_space=pltpu.VMEM),
        scratch_shapes=[
            pltpu.VMEM((4, 2, depth, columns), jnp.bfloat16),
            pltpu.VMEM((points, 4 * inner), jnp.bfloat16),
            dma((2, EARLY)), dma((2, EARLY)),
            dma((2, CHUNKS)), dma((2, CHUNKS)),
            dma((2, CHUNKS)), dma((2, CHUNKS)),
            dma((CHUNKS,)), dma((CHUNKS,)),
            dma((2, 3)), dma((2, 3)),
            dma((2,)),
        ],
        compiler_params=pltpu.CompilerParams(
            collective_id=0, has_side_effects=True, vmem_limit_bytes=20 * 2**20
        ),
        cost_estimate=pl.CostEstimate(
            flops=2 * points * 8 * depth * columns,
            bytes_accessed=2 * (points * columns + points * inner + depth * columns),
            transcendentals=0,
        ),
        name="gather_multiply",
    )(orbitals, rotation)


def with_collectives(orbitals, rotation):
    all_cols = lax.all_gather(orbitals, "band", axis=1, tiled=True)
    all_rows = lax.all_gather(rotation, "grid", axis=0, tiled=True)
    total = jnp.dot(all_cols, all_rows, preferred_element_type=jnp.float32)
    return total.astype(jnp.bfloat16)


def solution(mesh):
    specs = (P("grid", "band"), P("grid", "band"))

    def on_device(orbitals, rotation):
        square = mesh.shape["grid"] == 8 and mesh.shape["band"] == 4
        fits = (
            orbitals.shape[1] % 128 == 0
            and rotation.shape[0] % 64 == 0
            and rotation.shape[1] % (128 * CHUNKS) == 0
        )
        return (in_kernel if square and fits else with_collectives)(orbitals, rotation)

    return jax.shard_map(
        on_device, mesh=mesh, in_specs=specs, out_specs=P("grid", "band"), check_vma=False
    )
```

```python
import functools

import jax
import jax.numpy as jnp
from jax import lax
from jax.experimental import pallas as pl
from jax.experimental.pallas import tpu as pltpu
from jax.sharding import PartitionSpec as P

CHUNKS = 16
EARLY = 4
AHEAD = 5
LEFT = 4


def gather_multiply(
    orb_ref, rot_ref, out_ref, gathered, points,
    early_send, early_recv, late_send, late_recv,
    pair_send, pair_recv, line_send, line_recv, local_sem,
):
    depth, columns = rot_ref.shape
    inner = orb_ref.shape[1]
    half = depth // 2
    wide, narrow = columns // EARLY, columns // CHUNKS

    me = lax.axis_index("grid")
    z = lax.axis_index("band")
    nz = lax.axis_size("band")
    chip, core = me // 2, me % 2
    y, x = chip // 2, chip % 2
    chip_x = y * 2 + (1 - x)
    chip_y = (1 - y) * 2 + x
    chip_far = (1 - y) * 2 + (1 - x)
    sides = (chip_x, chip_y)

    def device(a_chip, a_core=core, a_z=z):
        return {"grid": a_chip * 2 + a_core, "band": a_z}

    first = (slice(0, half), slice(half, depth))

    def cols(j, width):
        return pl.ds(pl.multiple_of(j * width, width), width)

    def remote(src, dst, send, recv, to):
        return pltpu.make_async_remote_copy(
            src_ref=src, dst_ref=dst, send_sem=send, recv_sem=recv, device_id=to,
            device_id_type=pl.DeviceIdType.MESH,
        )

    def early(d, p):
        where = cols(p, wide)
        return remote(
            rot_ref.at[first[d], where], gathered.at[y, x, core, first[d], where],
            early_send.at[d, p], early_recv.at[d, p], device(sides[d]))

    def late(d, j):
        where = cols(j, narrow)
        if d == 0:
            ref = gathered.at[:, x, core, first[1], where]
        else:
            ref = gathered.at[y, :, core, first[0], where]
        return remote(ref, ref, late_send.at[d, j], late_recv.at[d, j], device(sides[d]))

    def pair(j):
        ref = gathered.at[:, :, core, :, cols(j, narrow)]
        return remote(ref, ref, pair_send.at[j], pair_recv.at[j], device(chip, 1 - core))

    def line(up, k):
        origin = z - k if up else z + k
        to = z + 1 if up else z - 1
        dst = points.at[:, pl.ds(pl.multiple_of(origin * inner, inner), inner)]
        d = 0 if up else 1
        return remote(
            orb_ref if k == 0 else dst, dst,
            line_send.at[d, k], line_recv.at[d, k], device(chip, core, to))

    def line_has(up, k):
        return (z >= k) & (z < nz - 1) if up else (z <= nz - 1 - k) & (z > 0)

    def line_gets(up, k):
        return z >= k + 1 if up else z <= nz - 2 - k

    def line_step(k):
        for up in (True, False):
            if k > 0:
                @pl.when(line_gets(up, k - 1))
                def _():
                    line(up, k - 1).wait_recv()
            if k < 3:
                @pl.when(line_has(up, k))
                def _():
                    line(up, k).start()

    barrier = pltpu.get_barrier_semaphore()

    def greet(to):
        pl.semaphore_signal(barrier, inc=1, device_id=to, device_id_type=pl.DeviceIdType.MESH)

    own_rot = pltpu.make_async_copy(rot_ref, gathered.at[y, x, core], local_sem.at[0])
    own_orb = pltpu.make_async_copy(
        orb_ref, points.at[:, pl.ds(pl.multiple_of(z * inner, inner), inner)], local_sem.at[1])
    own_rot.start()
    own_orb.start()

    for to in (device(chip_x), device(chip_y), device(chip, 1 - core)):
        greet(to)

    @pl.when(z > 0)
    def _():
        greet(device(chip, core, z - 1))

    @pl.when(z < nz - 1)
    def _():
        greet(device(chip, core, z + 1))

    middle = (z > 0) & (z < nz - 1)

    @pl.when(middle)
    def _():
        pl.semaphore_wait(barrier, 5)

    @pl.when(jnp.logical_not(middle))
    def _():
        pl.semaphore_wait(barrier, 4)

    def start_early(p):
        for d in (0, 1):
            early(d, p).start()

    def got_early(p):
        for d in (0, 1):
            early(d, p).wait_recv()

    def start_late(j):
        for d in (0, 1):
            late(d, j).start()

    def exchange(j):
        for d in (0, 1):
            late(d, j).wait_recv()
        pair(j).start()

    def multiply(j):
        pair(j).wait_recv()
        where = cols(j, narrow)
        block = gathered[:, :, :, :, where].reshape(8 * depth, narrow)
        out_ref[:, where] = jnp.dot(
            points[...], block, preferred_element_type=jnp.float32
        ).astype(out_ref.dtype)

    line_step(0)
    start_early(0)
    start_early(1)
    own_rot.wait()
    own_orb.wait()
    got_early(0)
    start_early(2)
    got_early(1)
    start_early(3)
    line_step(1)
    got_early(2)
    for j in range(3):
        start_late(j)
    got_early(3)
    for j in range(3, AHEAD):
        start_late(j)
    line_step(2)

    def receive(j, _):
        exchange(j)

        @pl.when(j + AHEAD < CHUNKS)
        def _():
            start_late(j + AHEAD)

        return 0

    lax.fori_loop(0, 4, receive, 0)
    line_step(3)

    def catch_up(j, _):
        receive(j, 0)

        def one(i, _):
            multiply(i)
            return 0

        lax.fori_loop(2 * (j - 4), 2 * (j - 4) + 2, one, 0)
        return 0

    lax.fori_loop(4, 8, catch_up, 0)
    receive(8, 0)

    def steady(j, _):
        receive(j, 0)
        multiply(j - 1)
        return 0

    lax.fori_loop(9, CHUNKS - LEFT + 1, steady, 0)

    def last(j, _):
        receive(j, 0)
        return 0

    lax.fori_loop(CHUNKS - LEFT + 1, CHUNKS, last, 0)

    def arrived(j, _):
        pair(j).wait_recv()
        return 0

    lax.fori_loop(CHUNKS - LEFT, CHUNKS, arrived, 0)

    for p in range(EARLY):
        for d in (0, 1):
            early(d, p).wait_send()

    def sent(j, _):
        for d in (0, 1):
            late(d, j).wait_send()
        pair(j).wait_send()
        return 0

    lax.fori_loop(0, CHUNKS, sent, 0)
    for k in range(3):
        for up in (True, False):
            @pl.when(line_has(up, k))
            def _():
                line(up, k).wait_send()


def write_rest(first_ref, gathered, points, out_ref, last, sems):
    rows, done = first_ref.shape
    columns = out_ref.shape[1]
    narrow = (columns - done) // LEFT
    depth = points.shape[1]
    block = rows // LEFT
    copies = []
    for i in range(LEFT):
        part = pl.ds(i * block, block)
        copies.append(pltpu.make_async_copy(
            first_ref.at[part], out_ref.at[part, pl.ds(0, done)], sems.at[i]))
        copies[-1].start()

    def put(i):
        start = pl.multiple_of(i * narrow, narrow)
        at = pl.multiple_of(done + i * narrow, narrow)
        return pltpu.make_async_copy(
            last.at[:, pl.ds(start, narrow)], out_ref.at[:, pl.ds(at, narrow)],
            sems.at[LEFT + i])

    def multiply(i, _):
        at = pl.ds(pl.multiple_of(done + i * narrow, narrow), narrow)
        where = pl.ds(pl.multiple_of(i * narrow, narrow), narrow)
        weights = gathered[:, :, :, :, at].reshape(depth, narrow)
        last[:, where] = jnp.dot(
            points[...], weights, preferred_element_type=jnp.float32
        ).astype(last.dtype)
        put(i).start()
        return 0

    lax.fori_loop(0, LEFT, multiply, 0)
    for copy in copies:
        copy.wait()
    for i in range(LEFT):
        put(i).wait()


def in_kernel(orbitals, rotation):
    points, inner = orbitals.shape
    depth, columns = rotation.shape
    bf16 = jnp.bfloat16
    rest = columns // CHUNKS * LEFT
    dma = pltpu.SemaphoreType.DMA
    vmem = pl.BlockSpec(memory_space=pltpu.VMEM)
    hbm = pl.BlockSpec(memory_space=pltpu.HBM)
    first, gathered, all_points = pl.pallas_call(
        gather_multiply,
        out_shape=(
            pltpu.VMEM((points, columns - rest), bf16),
            pltpu.VMEM((2, 2, 2, depth, columns), bf16),
            pltpu.VMEM((points, 4 * inner), bf16),
        ),
        in_specs=[hbm] * 2,
        out_specs=(vmem,) * 3,
        scratch_shapes=[
            dma((2, EARLY)), dma((2, EARLY)),
            dma((2, CHUNKS)), dma((2, CHUNKS)),
            dma((CHUNKS,)), dma((CHUNKS,)),
            dma((2, 3)), dma((2, 3)),
            dma((2,)),
        ],
        compiler_params=pltpu.CompilerParams(
            collective_id=0, has_side_effects=True, vmem_limit_bytes=16 * 2**20
        ),
        cost_estimate=pl.CostEstimate(
            flops=2 * points * 8 * depth * (columns - rest),
            bytes_accessed=2 * (points * inner + depth * columns),
            transcendentals=0,
        ),
        name="gather_multiply",
    )(
        pltpu.with_memory_space_constraint(orbitals, pltpu.HBM),
        pltpu.with_memory_space_constraint(rotation, pltpu.HBM),
    )
    keep = functools.partial(pltpu.with_memory_space_constraint, memory_space=pltpu.VMEM)
    return pl.pallas_call(
        write_rest,
        out_shape=pltpu.HBM((points, columns), bf16),
        in_specs=[vmem] * 3,
        out_specs=hbm,
        scratch_shapes=[pltpu.VMEM((points, rest), bf16), dma((2 * LEFT,))],
        compiler_params=pltpu.CompilerParams(vmem_limit_bytes=16 * 2**20),
        cost_estimate=pl.CostEstimate(
            flops=2 * points * 8 * depth * rest,
            bytes_accessed=2 * points * columns,
            transcendentals=0,
        ),
        name="write_rest",
    )(keep(first), keep(gathered), keep(all_points))


def with_collectives(orbitals, rotation):
    all_cols = lax.all_gather(orbitals, "band", axis=1, tiled=True)
    all_rows = lax.all_gather(rotation, "grid", axis=0, tiled=True)
    total = jnp.dot(all_cols, all_rows, preferred_element_type=jnp.float32)
    return total.astype(jnp.bfloat16)


def solution(mesh):
    specs = (P("grid", "band"), P("grid", "band"))

    def on_device(orbitals, rotation):
        square = mesh.shape["grid"] == 8 and mesh.shape["band"] == 4
        fits = (
            orbitals.shape[1] % 128 == 0
            and rotation.shape[0] % 64 == 0
            and rotation.shape[1] % (128 * CHUNKS) == 0
        )
        return (in_kernel if square and fits else with_collectives)(orbitals, rotation)

    return jax.shard_map(
        on_device, mesh=mesh, in_specs=specs, out_specs=P("grid", "band"), check_vma=False
    )
```

```python
import functools

import jax
import jax.numpy as jnp
from jax import lax
from jax.experimental import pallas as pl
from jax.experimental.pallas import tpu as pltpu
from jax.sharding import PartitionSpec as P

CHUNKS = 16
EARLY = 4
AHEAD = 8
LEFT = 2
BLOCKS = 8


def gather_multiply(
    orb_ref, rot_ref, out_ref, gathered, points,
    early_send, early_recv, late_send, late_recv,
    pair_send, pair_recv, line_send, line_recv, local_sem,
):
    depth, columns = rot_ref.shape
    inner = orb_ref.shape[1]
    half = depth // 2
    wide, narrow = columns // EARLY, columns // CHUNKS

    me = lax.axis_index("grid")
    z = lax.axis_index("band")
    nz = lax.axis_size("band")
    chip, core = me // 2, me % 2
    y, x = chip // 2, chip % 2
    chip_x = y * 2 + (1 - x)
    chip_y = (1 - y) * 2 + x
    chip_far = (1 - y) * 2 + (1 - x)
    sides = (chip_x, chip_y)

    def device(a_chip, a_core=core, a_z=z):
        return {"grid": a_chip * 2 + a_core, "band": a_z}

    first = (slice(0, half), slice(half, depth))

    def cols(j, width):
        return pl.ds(pl.multiple_of(j * width, width), width)

    def remote(src, dst, send, recv, to):
        return pltpu.make_async_remote_copy(
            src_ref=src, dst_ref=dst, send_sem=send, recv_sem=recv, device_id=to,
            device_id_type=pl.DeviceIdType.MESH,
        )

    def early(d, p):
        where = cols(p, wide)
        return remote(
            rot_ref.at[first[d], where], gathered.at[y, x, core, first[d], where],
            early_send.at[d, p], early_recv.at[d, p], device(sides[d]))

    def late(d, j):
        where = cols(j, narrow)
        if d == 0:
            ref = gathered.at[:, x, core, first[1], where]
        else:
            ref = gathered.at[y, :, core, first[0], where]
        return remote(ref, ref, late_send.at[d, j], late_recv.at[d, j], device(sides[d]))

    def pair(j):
        ref = gathered.at[:, :, core, :, cols(j, narrow)]
        return remote(ref, ref, pair_send.at[j], pair_recv.at[j], device(chip, 1 - core))

    def line(up, k):
        origin = z - k if up else z + k
        to = z + 1 if up else z - 1
        dst = points.at[:, pl.ds(pl.multiple_of(origin * inner, inner), inner)]
        d = 0 if up else 1
        return remote(
            orb_ref if k == 0 else dst, dst,
            line_send.at[d, k], line_recv.at[d, k], device(chip, core, to))

    def line_has(up, k):
        return (z >= k) & (z < nz - 1) if up else (z <= nz - 1 - k) & (z > 0)

    def line_gets(up, k):
        return z >= k + 1 if up else z <= nz - 2 - k

    def line_step(k):
        for up in (True, False):
            if k > 0:
                @pl.when(line_gets(up, k - 1))
                def _():
                    line(up, k - 1).wait_recv()
            if k < 3:
                @pl.when(line_has(up, k))
                def _():
                    line(up, k).start()

    barrier = pltpu.get_barrier_semaphore()

    def greet(to):
        pl.semaphore_signal(barrier, inc=1, device_id=to, device_id_type=pl.DeviceIdType.MESH)

    own_rot = pltpu.make_async_copy(rot_ref, gathered.at[y, x, core], local_sem.at[0])
    own_orb = pltpu.make_async_copy(
        orb_ref, points.at[:, pl.ds(pl.multiple_of(z * inner, inner), inner)], local_sem.at[1])
    own_rot.start()
    own_orb.start()

    for to in (device(chip_x), device(chip_y), device(chip, 1 - core)):
        greet(to)

    @pl.when(z > 0)
    def _():
        greet(device(chip, core, z - 1))

    @pl.when(z < nz - 1)
    def _():
        greet(device(chip, core, z + 1))

    middle = (z > 0) & (z < nz - 1)

    @pl.when(middle)
    def _():
        pl.semaphore_wait(barrier, 5)

    @pl.when(jnp.logical_not(middle))
    def _():
        pl.semaphore_wait(barrier, 4)

    def start_early(p):
        for d in (0, 1):
            early(d, p).start()

    def got_early(p):
        for d in (0, 1):
            early(d, p).wait_recv()

    def start_late(j):
        for d in (0, 1):
            late(d, j).start()

    def exchange(j):
        for d in (0, 1):
            late(d, j).wait_recv()
        pair(j).start()

    def multiply(j):
        pair(j).wait_recv()
        where = cols(j, narrow)
        block = gathered[:, :, :, :, where].reshape(8 * depth, narrow)
        out_ref[:, where] = jnp.dot(
            points[...], block, preferred_element_type=jnp.float32
        ).astype(out_ref.dtype)

    line_step(0)
    for p in range(3):
        start_early(p)
    own_rot.wait()
    own_orb.wait()
    got_early(0)
    start_early(3)
    got_early(1)
    for j in range(2):
        start_late(j)
    line_step(1)
    got_early(2)
    for j in range(2, 5):
        start_late(j)
    got_early(3)
    for j in range(5, AHEAD):
        start_late(j)
    line_step(2)

    def receive(j, _):
        exchange(j)

        @pl.when(j + AHEAD < CHUNKS)
        def _():
            start_late(j + AHEAD)

        return 0

    lax.fori_loop(0, 4, receive, 0)
    line_step(3)

    def catch_up(j, _):
        receive(j, 0)

        def one(i, _):
            multiply(i)
            return 0

        lax.fori_loop(2 * (j - 4), 2 * (j - 4) + 2, one, 0)
        return 0

    lax.fori_loop(4, 8, catch_up, 0)
    receive(8, 0)

    def steady(j, _):
        receive(j, 0)
        multiply(j - 1)
        return 0

    lax.fori_loop(9, CHUNKS - LEFT + 1, steady, 0)

    def last(j, _):
        receive(j, 0)
        return 0

    lax.fori_loop(CHUNKS - LEFT + 1, CHUNKS, last, 0)

    def arrived(j, _):
        pair(j).wait_recv()
        return 0

    lax.fori_loop(CHUNKS - LEFT, CHUNKS, arrived, 0)

    for p in range(EARLY):
        for d in (0, 1):
            early(d, p).wait_send()

    def sent(j, _):
        for d in (0, 1):
            late(d, j).wait_send()
        pair(j).wait_send()
        return 0

    lax.fori_loop(0, CHUNKS, sent, 0)
    for k in range(3):
        for up in (True, False):
            @pl.when(line_has(up, k))
            def _():
                line(up, k).wait_send()


def write_rest(first_ref, gathered, points, out_ref, last, sems):
    rows, done = first_ref.shape
    columns = out_ref.shape[1]
    narrow = (columns - done) // LEFT
    depth = points.shape[1]
    block = rows // BLOCKS
    copies = []
    for i in range(BLOCKS):
        part = pl.ds(i * block, block)
        copies.append(pltpu.make_async_copy(
            first_ref.at[part], out_ref.at[part, pl.ds(0, done)], sems.at[i]))
        copies[-1].start()

    def put(i):
        start = pl.multiple_of(i * narrow, narrow)
        at = pl.multiple_of(done + i * narrow, narrow)
        return pltpu.make_async_copy(
            last.at[:, pl.ds(start, narrow)], out_ref.at[:, pl.ds(at, narrow)],
            sems.at[BLOCKS + i])

    def multiply(i, _):
        at = pl.ds(pl.multiple_of(done + i * narrow, narrow), narrow)
        where = pl.ds(pl.multiple_of(i * narrow, narrow), narrow)
        weights = gathered[:, :, :, :, at].reshape(depth, narrow)
        last[:, where] = jnp.dot(
            points[...], weights, preferred_element_type=jnp.float32
        ).astype(last.dtype)
        put(i).start()
        return 0

    lax.fori_loop(0, LEFT, multiply, 0)
    for copy in copies:
        copy.wait()
    for i in range(LEFT):
        put(i).wait()


def in_kernel(orbitals, rotation):
    points, inner = orbitals.shape
    depth, columns = rotation.shape
    bf16 = jnp.bfloat16
    rest = columns // CHUNKS * LEFT
    dma = pltpu.SemaphoreType.DMA
    vmem = pl.BlockSpec(memory_space=pltpu.VMEM)
    hbm = pl.BlockSpec(memory_space=pltpu.HBM)
    first, gathered, all_points = pl.pallas_call(
        gather_multiply,
        out_shape=(
            pltpu.VMEM((points, columns - rest), bf16),
            pltpu.VMEM((2, 2, 2, depth, columns), bf16),
            pltpu.VMEM((points, 4 * inner), bf16),
        ),
        in_specs=[hbm] * 2,
        out_specs=(vmem,) * 3,
        scratch_shapes=[
            dma((2, EARLY)), dma((2, EARLY)),
            dma((2, CHUNKS)), dma((2, CHUNKS)),
            dma((CHUNKS,)), dma((CHUNKS,)),
            dma((2, 3)), dma((2, 3)),
            dma((2,)),
        ],
        compiler_params=pltpu.CompilerParams(
            collective_id=0, has_side_effects=True, vmem_limit_bytes=16 * 2**20
        ),
        cost_estimate=pl.CostEstimate(
            flops=2 * points * 8 * depth * (columns - rest),
            bytes_accessed=2 * (points * inner + depth * columns),
            transcendentals=0,
        ),
        name="gather_multiply",
    )(
        pltpu.with_memory_space_constraint(orbitals, pltpu.HBM),
        pltpu.with_memory_space_constraint(rotation, pltpu.HBM),
    )
    keep = functools.partial(pltpu.with_memory_space_constraint, memory_space=pltpu.VMEM)
    return pl.pallas_call(
        write_rest,
        out_shape=pltpu.HBM((points, columns), bf16),
        in_specs=[vmem] * 3,
        out_specs=hbm,
        scratch_shapes=[pltpu.VMEM((points, rest), bf16), dma((BLOCKS + LEFT,))],
        compiler_params=pltpu.CompilerParams(vmem_limit_bytes=16 * 2**20),
        cost_estimate=pl.CostEstimate(
            flops=2 * points * 8 * depth * rest,
            bytes_accessed=2 * points * columns,
            transcendentals=0,
        ),
        name="write_rest",
    )(keep(first), keep(gathered), keep(all_points))


def with_collectives(orbitals, rotation):
    all_cols = lax.all_gather(orbitals, "band", axis=1, tiled=True)
    all_rows = lax.all_gather(rotation, "grid", axis=0, tiled=True)
    total = jnp.dot(all_cols, all_rows, preferred_element_type=jnp.float32)
    return total.astype(jnp.bfloat16)


def solution(mesh):
    specs = (P("grid", "band"), P("grid", "band"))

    def on_device(orbitals, rotation):
        square = mesh.shape["grid"] == 8 and mesh.shape["band"] == 4
        fits = (
            orbitals.shape[1] % 128 == 0
            and rotation.shape[0] % 64 == 0
            and rotation.shape[1] % (128 * CHUNKS) == 0
        )
        return (in_kernel if square and fits else with_collectives)(orbitals, rotation)

    return jax.shard_map(
        on_device, mesh=mesh, in_specs=specs, out_specs=P("grid", "band"), check_vma=False
    )
```

```python
import functools

import jax
import jax.numpy as jnp
from jax import lax
from jax.experimental import pallas as pl
from jax.experimental.pallas import tpu as pltpu
from jax.sharding import PartitionSpec as P

CHUNKS = 16
GROUP = 4
AHEAD = 5
LEFT = 4
BLOCKS = 8


def gather_multiply(
    orb_ref, rot_ref, out_ref, gathered, points,
    early_send, early_recv, late_send, late_recv,
    pair_send, pair_recv, line_send, line_recv, own_sem, local_sem,
):
    depth, columns = rot_ref.shape
    inner = orb_ref.shape[1]
    half = depth // 2
    narrow = columns // CHUNKS

    me = lax.axis_index("grid")
    z = lax.axis_index("band")
    nz = lax.axis_size("band")
    chip, core = me // 2, me % 2
    y, x = chip // 2, chip % 2
    chip_x = y * 2 + (1 - x)
    chip_y = (1 - y) * 2 + x
    chip_far = (1 - y) * 2 + (1 - x)
    sides = (chip_x, chip_y)

    def device(a_chip, a_core=core, a_z=z):
        return {"grid": a_chip * 2 + a_core, "band": a_z}

    first = (slice(0, half), slice(half, depth))

    def cols(j, width):
        return pl.ds(pl.multiple_of(j * width, width), width)

    def remote(src, dst, send, recv, to):
        return pltpu.make_async_remote_copy(
            src_ref=src, dst_ref=dst, send_sem=send, recv_sem=recv, device_id=to,
            device_id_type=pl.DeviceIdType.MESH,
        )

    def early(d, p):
        where = cols(p, narrow)
        return remote(
            rot_ref.at[first[d], where], gathered.at[p, y, x, core, first[d]],
            early_send.at[d, p], early_recv.at[d, p], device(sides[d]))

    def late(d, j):
        if d == 0:
            ref = gathered.at[j, :, x, core, first[1]]
        else:
            ref = gathered.at[j, y, :, core, first[0]]
        return remote(ref, ref, late_send.at[d, j], late_recv.at[d, j], device(sides[d]))

    def pair(j):
        ref = gathered.at[j, :, :, core]
        return remote(ref, ref, pair_send.at[j], pair_recv.at[j], device(chip, 1 - core))

    def line(up, k):
        origin = z - k if up else z + k
        to = z + 1 if up else z - 1
        dst = points.at[:, pl.ds(pl.multiple_of(origin * inner, inner), inner)]
        d = 0 if up else 1
        return remote(
            orb_ref if k == 0 else dst, dst,
            line_send.at[d, k], line_recv.at[d, k], device(chip, core, to))

    def line_has(up, k):
        return (z >= k) & (z < nz - 1) if up else (z <= nz - 1 - k) & (z > 0)

    def line_gets(up, k):
        return z >= k + 1 if up else z <= nz - 2 - k

    def line_step(k):
        for up in (True, False):
            if k > 0:
                @pl.when(line_gets(up, k - 1))
                def _():
                    line(up, k - 1).wait_recv()
            if k < 3:
                @pl.when(line_has(up, k))
                def _():
                    line(up, k).start()

    barrier = pltpu.get_barrier_semaphore()

    def greet(to):
        pl.semaphore_signal(barrier, inc=1, device_id=to, device_id_type=pl.DeviceIdType.MESH)

    def own_rot(j):
        return pltpu.make_async_copy(
            rot_ref.at[:, cols(j, narrow)], gathered.at[j, y, x, core], own_sem.at[j])

    def each(function, start, stop):
        def one(j, _):
            function(j)
            return 0

        lax.fori_loop(start, stop, one, 0)

    own_orb = pltpu.make_async_copy(
        orb_ref, points.at[:, pl.ds(pl.multiple_of(z * inner, inner), inner)], local_sem)
    each(lambda j: own_rot(j).start(), 0, CHUNKS)
    own_orb.start()

    for to in (device(chip_x), device(chip_y), device(chip, 1 - core)):
        greet(to)

    @pl.when(z > 0)
    def _():
        greet(device(chip, core, z - 1))

    @pl.when(z < nz - 1)
    def _():
        greet(device(chip, core, z + 1))

    middle = (z > 0) & (z < nz - 1)

    @pl.when(middle)
    def _():
        pl.semaphore_wait(barrier, 5)

    @pl.when(jnp.logical_not(middle))
    def _():
        pl.semaphore_wait(barrier, 4)

    def start_early(group):
        def one(p):
            for d in (0, 1):
                early(d, p).start()

        each(one, group * GROUP, (group + 1) * GROUP)

    def got_early(group):
        def one(p):
            for d in (0, 1):
                early(d, p).wait_recv()

        each(one, group * GROUP, (group + 1) * GROUP)

    def start_late(j):
        for d in (0, 1):
            late(d, j).start()

    def exchange(j):
        for d in (0, 1):
            late(d, j).wait_recv()
        pair(j).start()

    def multiply(j):
        pair(j).wait_recv()
        where = cols(j, narrow)
        block = gathered[j].reshape(8 * depth, narrow)
        out_ref[:, where] = jnp.dot(
            points[...], block, preferred_element_type=jnp.float32
        ).astype(out_ref.dtype)

    line_step(0)
    start_early(0)
    start_early(1)
    each(lambda j: own_rot(j).wait(), 0, CHUNKS)
    own_orb.wait()
    got_early(0)
    start_early(2)
    got_early(1)
    start_early(3)
    line_step(1)
    got_early(2)
    for j in range(3):
        start_late(j)
    got_early(3)
    for j in range(3, AHEAD):
        start_late(j)
    line_step(2)

    def receive(j, _):
        exchange(j)

        @pl.when(j + AHEAD < CHUNKS)
        def _():
            start_late(j + AHEAD)

        return 0

    lax.fori_loop(0, 4, receive, 0)
    line_step(3)

    def catch_up(j, _):
        receive(j, 0)

        def one(i, _):
            multiply(i)
            return 0

        lax.fori_loop(2 * (j - 4), 2 * (j - 4) + 2, one, 0)
        return 0

    lax.fori_loop(4, 8, catch_up, 0)
    receive(8, 0)

    def steady(j, _):
        receive(j, 0)
        multiply(j - 1)
        return 0

    lax.fori_loop(9, CHUNKS - LEFT + 1, steady, 0)

    def last(j, _):
        receive(j, 0)
        return 0

    lax.fori_loop(CHUNKS - LEFT + 1, CHUNKS, last, 0)

    def arrived(j, _):
        pair(j).wait_recv()
        return 0

    lax.fori_loop(CHUNKS - LEFT, CHUNKS, arrived, 0)

    def sent(j, _):
        for d in (0, 1):
            early(d, j).wait_send()
            late(d, j).wait_send()
        pair(j).wait_send()
        return 0

    lax.fori_loop(0, CHUNKS, sent, 0)
    for k in range(3):
        for up in (True, False):
            @pl.when(line_has(up, k))
            def _():
                line(up, k).wait_send()


def write_rest(first_ref, gathered, points, out_ref, last, sems):
    rows, done = first_ref.shape
    columns = out_ref.shape[1]
    narrow = (columns - done) // LEFT
    depth = points.shape[1]
    block = rows // BLOCKS
    copies = []
    for i in range(BLOCKS):
        part = pl.ds(i * block, block)
        copies.append(pltpu.make_async_copy(
            first_ref.at[part], out_ref.at[part, pl.ds(0, done)], sems.at[i]))
        copies[-1].start(priority=i % 2)

    def put(i):
        start = pl.multiple_of(i * narrow, narrow)
        at = pl.multiple_of(done + i * narrow, narrow)
        return pltpu.make_async_copy(
            last.at[:, pl.ds(start, narrow)], out_ref.at[:, pl.ds(at, narrow)],
            sems.at[BLOCKS + i])

    def multiply(i, _):
        where = pl.ds(pl.multiple_of(i * narrow, narrow), narrow)
        weights = gathered[CHUNKS - LEFT + i].reshape(depth, narrow)
        last[:, where] = jnp.dot(
            points[...], weights, preferred_element_type=jnp.float32
        ).astype(last.dtype)
        put(i).start()
        return 0

    lax.fori_loop(0, LEFT, multiply, 0)
    for copy in copies:
        copy.wait()
    for i in range(LEFT):
        put(i).wait()


def in_kernel(orbitals, rotation):
    points, inner = orbitals.shape
    depth, columns = rotation.shape
    bf16 = jnp.bfloat16
    rest = columns // CHUNKS * LEFT
    dma = pltpu.SemaphoreType.DMA
    vmem = pl.BlockSpec(memory_space=pltpu.VMEM)
    hbm = pl.BlockSpec(memory_space=pltpu.HBM)
    first, gathered, all_points = pl.pallas_call(
        gather_multiply,
        out_shape=(
            pltpu.VMEM((points, columns - rest), bf16),
            pltpu.VMEM((CHUNKS, 2, 2, 2, depth, columns // CHUNKS), bf16),
            pltpu.VMEM((points, 4 * inner), bf16),
        ),
        in_specs=[hbm] * 2,
        out_specs=(vmem,) * 3,
        scratch_shapes=[
            dma((2, CHUNKS)), dma((2, CHUNKS)),
            dma((2, CHUNKS)), dma((2, CHUNKS)),
            dma((CHUNKS,)), dma((CHUNKS,)),
            dma((2, 3)), dma((2, 3)),
            dma((CHUNKS,)), dma,
        ],
        compiler_params=pltpu.CompilerParams(
            collective_id=0, has_side_effects=True, vmem_limit_bytes=16 * 2**20
        ),
        cost_estimate=pl.CostEstimate(
            flops=2 * points * 8 * depth * (columns - rest),
            bytes_accessed=2 * (points * inner + depth * columns),
            transcendentals=0,
        ),
        name="gather_multiply",
    )(
        pltpu.with_memory_space_constraint(orbitals, pltpu.HBM),
        pltpu.with_memory_space_constraint(rotation, pltpu.HBM),
    )
    keep = functools.partial(pltpu.with_memory_space_constraint, memory_space=pltpu.VMEM)
    return pl.pallas_call(
        write_rest,
        out_shape=pltpu.HBM((points, columns), bf16),
        in_specs=[vmem] * 3,
        out_specs=hbm,
        scratch_shapes=[pltpu.VMEM((points, rest), bf16), dma((BLOCKS + LEFT,))],
        compiler_params=pltpu.CompilerParams(vmem_limit_bytes=16 * 2**20),
        cost_estimate=pl.CostEstimate(
            flops=2 * points * 8 * depth * rest,
            bytes_accessed=2 * points * columns,
            transcendentals=0,
        ),
        name="write_rest",
    )(keep(first), keep(gathered), keep(all_points))


def with_collectives(orbitals, rotation):
    all_cols = lax.all_gather(orbitals, "band", axis=1, tiled=True)
    all_rows = lax.all_gather(rotation, "grid", axis=0, tiled=True)
    total = jnp.dot(all_cols, all_rows, preferred_element_type=jnp.float32)
    return total.astype(jnp.bfloat16)


def solution(mesh):
    specs = (P("grid", "band"), P("grid", "band"))

    def on_device(orbitals, rotation):
        square = mesh.shape["grid"] == 8 and mesh.shape["band"] == 4
        fits = (
            orbitals.shape[1] % 128 == 0
            and rotation.shape[0] % 64 == 0
            and rotation.shape[1] % (128 * CHUNKS) == 0
        )
        return (in_kernel if square and fits else with_collectives)(orbitals, rotation)

    return jax.shard_map(
        on_device, mesh=mesh, in_specs=specs, out_specs=P("grid", "band"), check_vma=False
    )
```

```python
import functools

import jax
import jax.numpy as jnp
from jax import lax
from jax.experimental import pallas as pl
from jax.experimental.pallas import tpu as pltpu
from jax.sharding import PartitionSpec as P

CHUNKS = 16
EARLY = 4
AHEAD = 5
LEFT = 5
BLOCKS = 4


def gather_multiply(
    orb_ref, rot_ref, out_ref, gathered, points,
    early_send, early_recv, late_send, late_recv,
    pair_send, pair_recv, line_send, line_recv, local_sem,
):
    depth, columns = rot_ref.shape
    inner = orb_ref.shape[1]
    half = depth // 2
    wide, narrow = columns // EARLY, columns // CHUNKS

    me = lax.axis_index("grid")
    z = lax.axis_index("band")
    nz = lax.axis_size("band")
    chip, core = me // 2, me % 2
    y, x = chip // 2, chip % 2
    chip_x = y * 2 + (1 - x)
    chip_y = (1 - y) * 2 + x
    chip_far = (1 - y) * 2 + (1 - x)
    sides = (chip_x, chip_y)

    def device(a_chip, a_core=core, a_z=z):
        return {"grid": a_chip * 2 + a_core, "band": a_z}

    first = (slice(0, half), slice(half, depth))

    def cols(j, width):
        return pl.ds(pl.multiple_of(j * width, width), width)

    def remote(src, dst, send, recv, to):
        return pltpu.make_async_remote_copy(
            src_ref=src, dst_ref=dst, send_sem=send, recv_sem=recv, device_id=to,
            device_id_type=pl.DeviceIdType.MESH,
        )

    def early(d, p):
        where = cols(p, wide)
        return remote(
            rot_ref.at[first[d], where], gathered.at[y, x, core, first[d], where],
            early_send.at[d, p], early_recv.at[d, p], device(sides[d]))

    def late(d, j):
        where = cols(j, narrow)
        if d == 0:
            ref = gathered.at[:, x, core, first[1], where]
        else:
            ref = gathered.at[y, :, core, first[0], where]
        return remote(ref, ref, late_send.at[d, j], late_recv.at[d, j], device(sides[d]))

    def pair(j):
        ref = gathered.at[:, :, core, :, cols(j, narrow)]
        return remote(ref, ref, pair_send.at[j], pair_recv.at[j], device(chip, 1 - core))

    def line(up, k):
        origin = z - k if up else z + k
        to = z + 1 if up else z - 1
        dst = points.at[:, pl.ds(pl.multiple_of(origin * inner, inner), inner)]
        d = 0 if up else 1
        return remote(
            orb_ref if k == 0 else dst, dst,
            line_send.at[d, k], line_recv.at[d, k], device(chip, core, to))

    def line_has(up, k):
        return (z >= k) & (z < nz - 1) if up else (z <= nz - 1 - k) & (z > 0)

    def line_gets(up, k):
        return z >= k + 1 if up else z <= nz - 2 - k

    def line_step(k):
        for up in (True, False):
            if k > 0:
                @pl.when(line_gets(up, k - 1))
                def _():
                    line(up, k - 1).wait_recv()
            if k < 3:
                @pl.when(line_has(up, k))
                def _():
                    line(up, k).start()

    barrier = pltpu.get_barrier_semaphore()

    def greet(to):
        pl.semaphore_signal(barrier, inc=1, device_id=to, device_id_type=pl.DeviceIdType.MESH)

    own_rot = pltpu.make_async_copy(rot_ref, gathered.at[y, x, core], local_sem.at[0])
    own_orb = pltpu.make_async_copy(
        orb_ref, points.at[:, pl.ds(pl.multiple_of(z * inner, inner), inner)], local_sem.at[1])

    for to in (device(chip_x), device(chip_y), device(chip, 1 - core)):
        greet(to)

    @pl.when(z > 0)
    def _():
        greet(device(chip, core, z - 1))

    @pl.when(z < nz - 1)
    def _():
        greet(device(chip, core, z + 1))

    own_rot.start()
    own_orb.start()
    middle = (z > 0) & (z < nz - 1)

    @pl.when(middle)
    def _():
        pl.semaphore_wait(barrier, 5)

    @pl.when(jnp.logical_not(middle))
    def _():
        pl.semaphore_wait(barrier, 4)

    def start_early(p):
        for d in (0, 1):
            early(d, p).start()

    def got_early(p):
        for d in (0, 1):
            early(d, p).wait_recv()

    def start_late(j):
        for d in (0, 1):
            late(d, j).start()

    def exchange(j):
        for d in (0, 1):
            late(d, j).wait_recv()
        pair(j).start()

    def multiply(j):
        pair(j).wait_recv()
        where = cols(j, narrow)
        block = gathered[:, :, :, :, where].reshape(8 * depth, narrow)
        out_ref[:, where] = jnp.dot(
            points[...], block, preferred_element_type=jnp.float32
        ).astype(out_ref.dtype)

    start_early(0)
    line_step(0)
    start_early(1)
    own_rot.wait()
    own_orb.wait()
    got_early(0)
    start_early(2)
    got_early(1)
    start_early(3)
    line_step(1)
    got_early(2)
    for j in range(3):
        start_late(j)
    got_early(3)
    for j in range(3, AHEAD):
        start_late(j)
    line_step(2)

    def receive(j, _):
        exchange(j)

        @pl.when(j + AHEAD < CHUNKS)
        def _():
            start_late(j + AHEAD)

        return 0

    lax.fori_loop(0, 4, receive, 0)
    line_step(3)

    def catch_up(j, _):
        receive(j, 0)

        def one(i, _):
            multiply(i)
            return 0

        lax.fori_loop(2 * (j - 4), 2 * (j - 4) + 2, one, 0)
        return 0

    lax.fori_loop(4, 8, catch_up, 0)
    receive(8, 0)

    def steady(j, _):
        receive(j, 0)
        multiply(j - 1)
        return 0

    lax.fori_loop(9, CHUNKS - LEFT + 1, steady, 0)

    def last(j, _):
        receive(j, 0)
        return 0

    lax.fori_loop(CHUNKS - LEFT + 1, CHUNKS, last, 0)

    def arrived(j, _):
        pair(j).wait_recv()
        return 0

    lax.fori_loop(CHUNKS - LEFT, CHUNKS, arrived, 0)

    for p in range(EARLY):
        for d in (0, 1):
            early(d, p).wait_send()

    def sent(j, _):
        for d in (0, 1):
            late(d, j).wait_send()
        pair(j).wait_send()
        return 0

    lax.fori_loop(0, CHUNKS, sent, 0)
    for k in range(3):
        for up in (True, False):
            @pl.when(line_has(up, k))
            def _():
                line(up, k).wait_send()


def write_rest(first_ref, gathered, points, out_ref, last, sems):
    rows, done = first_ref.shape
    columns = out_ref.shape[1]
    narrow = (columns - done) // LEFT
    depth = points.shape[1]
    block = rows // BLOCKS
    copies = []
    for i in range(BLOCKS):
        part = pl.ds(i * block, block)
        copies.append(pltpu.make_async_copy(
            first_ref.at[part], out_ref.at[part, pl.ds(0, done)], sems.at[i]))
        copies[-1].start()

    def put(i):
        start = pl.multiple_of(i * narrow, narrow)
        at = pl.multiple_of(done + i * narrow, narrow)
        return pltpu.make_async_copy(
            last.at[:, pl.ds(start, narrow)], out_ref.at[:, pl.ds(at, narrow)],
            sems.at[BLOCKS + i])

    def multiply(i, _):
        at = pl.ds(pl.multiple_of(done + i * narrow, narrow), narrow)
        where = pl.ds(pl.multiple_of(i * narrow, narrow), narrow)
        weights = gathered[:, :, :, :, at].reshape(depth, narrow)
        last[:, where] = jnp.dot(
            points[...], weights, preferred_element_type=jnp.float32
        ).astype(last.dtype)
        put(i).start()
        return 0

    lax.fori_loop(0, LEFT, multiply, 0)
    for copy in copies:
        copy.wait()
    for i in range(LEFT):
        put(i).wait()


def in_kernel(orbitals, rotation):
    points, inner = orbitals.shape
    depth, columns = rotation.shape
    bf16 = jnp.bfloat16
    rest = columns // CHUNKS * LEFT
    dma = pltpu.SemaphoreType.DMA
    vmem = pl.BlockSpec(memory_space=pltpu.VMEM)
    hbm = pl.BlockSpec(memory_space=pltpu.HBM)
    first, gathered, all_points = pl.pallas_call(
        gather_multiply,
        out_shape=(
            pltpu.VMEM((points, columns - rest), bf16),
            pltpu.VMEM((2, 2, 2, depth, columns), bf16),
            pltpu.VMEM((points, 4 * inner), bf16),
        ),
        in_specs=[hbm] * 2,
        out_specs=(vmem,) * 3,
        scratch_shapes=[
            dma((2, EARLY)), dma((2, EARLY)),
            dma((2, CHUNKS)), dma((2, CHUNKS)),
            dma((CHUNKS,)), dma((CHUNKS,)),
            dma((2, 3)), dma((2, 3)),
            dma((2,)),
        ],
        compiler_params=pltpu.CompilerParams(
            collective_id=0, has_side_effects=True, vmem_limit_bytes=16 * 2**20
        ),
        cost_estimate=pl.CostEstimate(
            flops=2 * points * 8 * depth * (columns - rest),
            bytes_accessed=2 * (points * inner + depth * columns),
            transcendentals=0,
        ),
        name="gather_multiply",
    )(
        pltpu.with_memory_space_constraint(orbitals, pltpu.HBM),
        pltpu.with_memory_space_constraint(rotation, pltpu.HBM),
    )
    keep = functools.partial(pltpu.with_memory_space_constraint, memory_space=pltpu.VMEM)
    return pl.pallas_call(
        write_rest,
        out_shape=pltpu.HBM((points, columns), bf16),
        in_specs=[vmem] * 3,
        out_specs=hbm,
        scratch_shapes=[pltpu.VMEM((points, rest), bf16), dma((BLOCKS + LEFT,))],
        compiler_params=pltpu.CompilerParams(vmem_limit_bytes=16 * 2**20),
        cost_estimate=pl.CostEstimate(
            flops=2 * points * 8 * depth * rest,
            bytes_accessed=2 * points * columns,
            transcendentals=0,
        ),
        name="write_rest",
    )(keep(first), keep(gathered), keep(all_points))


def with_collectives(orbitals, rotation):
    all_cols = lax.all_gather(orbitals, "band", axis=1, tiled=True)
    all_rows = lax.all_gather(rotation, "grid", axis=0, tiled=True)
    total = jnp.dot(all_cols, all_rows, preferred_element_type=jnp.float32)
    return total.astype(jnp.bfloat16)


def solution(mesh):
    specs = (P("grid", "band"), P("grid", "band"))

    def on_device(orbitals, rotation):
        square = mesh.shape["grid"] == 8 and mesh.shape["band"] == 4
        fits = (
            orbitals.shape[1] % 128 == 0
            and rotation.shape[0] % 64 == 0
            and rotation.shape[1] % (128 * CHUNKS) == 0
        )
        return (in_kernel if square and fits else with_collectives)(orbitals, rotation)

    return jax.shard_map(
        on_device, mesh=mesh, in_specs=specs, out_specs=P("grid", "band"), check_vma=False
    )
```

```python
import functools

import jax
import jax.numpy as jnp
from jax import lax
from jax.experimental import pallas as pl
from jax.experimental.pallas import tpu as pltpu
from jax.sharding import PartitionSpec as P

CHUNKS = 16
EARLY = 4
AHEAD = 3
LEFT = 5
BLOCKS = 4


def gather_multiply(
    orb_ref, rot_ref, out_ref, gathered, points,
    early_send, early_recv, late_send, late_recv,
    pair_send, pair_recv, line_send, line_recv, local_sem,
):
    depth, columns = rot_ref.shape
    inner = orb_ref.shape[1]
    half = depth // 2
    wide, narrow = columns // EARLY, columns // CHUNKS

    me = lax.axis_index("grid")
    z = lax.axis_index("band")
    nz = lax.axis_size("band")
    chip, core = me // 2, me % 2
    y, x = chip // 2, chip % 2
    chip_x = y * 2 + (1 - x)
    chip_y = (1 - y) * 2 + x
    chip_far = (1 - y) * 2 + (1 - x)
    sides = (chip_x, chip_y)

    def device(a_chip, a_core=core, a_z=z):
        return {"grid": a_chip * 2 + a_core, "band": a_z}

    first = (slice(0, half), slice(half, depth))

    def cols(j, width):
        return pl.ds(pl.multiple_of(j * width, width), width)

    def remote(src, dst, send, recv, to):
        return pltpu.make_async_remote_copy(
            src_ref=src, dst_ref=dst, send_sem=send, recv_sem=recv, device_id=to,
            device_id_type=pl.DeviceIdType.MESH,
        )

    def early(d, p):
        where = cols(p, wide)
        return remote(
            rot_ref.at[first[d], where], gathered.at[y, x, core, first[d], where],
            early_send.at[d, p], early_recv.at[d, p], device(sides[d]))

    def late(d, j):
        where = cols(j, narrow)
        if d == 0:
            ref = gathered.at[:, x, core, first[1], where]
        else:
            ref = gathered.at[y, :, core, first[0], where]
        return remote(ref, ref, late_send.at[d, j], late_recv.at[d, j], device(sides[d]))

    def pair(j):
        ref = gathered.at[:, :, core, :, cols(j, narrow)]
        return remote(ref, ref, pair_send.at[j], pair_recv.at[j], device(chip, 1 - core))

    def line(up, k):
        origin = z - k if up else z + k
        to = z + 1 if up else z - 1
        dst = points.at[:, pl.ds(pl.multiple_of(origin * inner, inner), inner)]
        d = 0 if up else 1
        return remote(
            orb_ref if k == 0 else dst, dst,
            line_send.at[d, k], line_recv.at[d, k], device(chip, core, to))

    def line_has(up, k):
        return (z >= k) & (z < nz - 1) if up else (z <= nz - 1 - k) & (z > 0)

    def line_gets(up, k):
        return z >= k + 1 if up else z <= nz - 2 - k

    def line_step(k):
        for up in (True, False):
            if k > 0:
                @pl.when(line_gets(up, k - 1))
                def _():
                    line(up, k - 1).wait_recv()
            if k < 3:
                @pl.when(line_has(up, k))
                def _():
                    line(up, k).start()

    barrier = pltpu.get_barrier_semaphore()

    def greet(to):
        pl.semaphore_signal(barrier, inc=1, device_id=to, device_id_type=pl.DeviceIdType.MESH)

    own_rot = pltpu.make_async_copy(rot_ref, gathered.at[y, x, core], local_sem.at[0])
    own_orb = pltpu.make_async_copy(
        orb_ref, points.at[:, pl.ds(pl.multiple_of(z * inner, inner), inner)], local_sem.at[1])

    for to in (device(chip_x), device(chip_y), device(chip, 1 - core)):
        greet(to)

    @pl.when(z > 0)
    def _():
        greet(device(chip, core, z - 1))

    @pl.when(z < nz - 1)
    def _():
        greet(device(chip, core, z + 1))

    own_rot.start()
    own_orb.start()
    middle = (z > 0) & (z < nz - 1)

    @pl.when(middle)
    def _():
        pl.semaphore_wait(barrier, 5)

    @pl.when(jnp.logical_not(middle))
    def _():
        pl.semaphore_wait(barrier, 4)

    def start_early(p):
        for d in (0, 1):
            early(d, p).start()

    def got_early(p):
        for d in (0, 1):
            early(d, p).wait_recv()

    def start_late(j):
        for d in (0, 1):
            late(d, j).start()

    def exchange(j):
        for d in (0, 1):
            late(d, j).wait_recv()
        pair(j).start()

    def multiply(j):
        pair(j).wait_recv()
        where = cols(j, narrow)
        block = gathered[:, :, :, :, where].reshape(8 * depth, narrow)
        out_ref[:, where] = jnp.dot(
            points[...], block, preferred_element_type=jnp.float32
        ).astype(out_ref.dtype)

    start_early(0)
    line_step(0)
    start_early(1)
    own_rot.wait()
    own_orb.wait()
    got_early(0)
    start_early(2)
    got_early(1)
    start_early(3)
    line_step(1)
    got_early(2)
    for j in range(3):
        start_late(j)
    got_early(3)
    for j in range(3, AHEAD):
        start_late(j)
    line_step(2)

    def receive(j, _):
        exchange(j)

        @pl.when(j + AHEAD < CHUNKS)
        def _():
            start_late(j + AHEAD)

        return 0

    lax.fori_loop(0, 4, receive, 0)
    line_step(3)

    def catch_up(j, _):
        receive(j, 0)

        def one(i, _):
            multiply(i)
            return 0

        lax.fori_loop(2 * (j - 4), 2 * (j - 4) + 2, one, 0)
        return 0

    lax.fori_loop(4, 8, catch_up, 0)
    receive(8, 0)

    def steady(j, _):
        receive(j, 0)
        multiply(j - 1)
        return 0

    lax.fori_loop(9, CHUNKS - LEFT + 1, steady, 0)

    def last(j, _):
        receive(j, 0)
        return 0

    lax.fori_loop(CHUNKS - LEFT + 1, CHUNKS, last, 0)

    def arrived(j, _):
        pair(j).wait_recv()
        return 0

    lax.fori_loop(CHUNKS - LEFT, CHUNKS, arrived, 0)

    for p in range(EARLY):
        for d in (0, 1):
            early(d, p).wait_send()

    def sent(j, _):
        for d in (0, 1):
            late(d, j).wait_send()
        pair(j).wait_send()
        return 0

    lax.fori_loop(0, CHUNKS, sent, 0)
    for k in range(3):
        for up in (True, False):
            @pl.when(line_has(up, k))
            def _():
                line(up, k).wait_send()


def write_rest(first_ref, gathered, points, out_ref, last, sems):
    rows, done = first_ref.shape
    columns = out_ref.shape[1]
    narrow = (columns - done) // LEFT
    depth = points.shape[1]
    block = rows // BLOCKS
    copies = []
    for i in range(BLOCKS):
        part = pl.ds(i * block, block)
        copies.append(pltpu.make_async_copy(
            first_ref.at[part], out_ref.at[part, pl.ds(0, done)], sems.at[i]))
        copies[-1].start()

    def put(i):
        start = pl.multiple_of(i * narrow, narrow)
        at = pl.multiple_of(done + i * narrow, narrow)
        return pltpu.make_async_copy(
            last.at[:, pl.ds(start, narrow)], out_ref.at[:, pl.ds(at, narrow)],
            sems.at[BLOCKS + i])

    def multiply(i, _):
        at = pl.ds(pl.multiple_of(done + i * narrow, narrow), narrow)
        where = pl.ds(pl.multiple_of(i * narrow, narrow), narrow)
        weights = gathered[:, :, :, :, at].reshape(depth, narrow)
        last[:, where] = jnp.dot(
            points[...], weights, preferred_element_type=jnp.float32
        ).astype(last.dtype)
        put(i).start()
        return 0

    lax.fori_loop(0, LEFT, multiply, 0)
    for copy in copies:
        copy.wait()
    for i in range(LEFT):
        put(i).wait()


def in_kernel(orbitals, rotation):
    points, inner = orbitals.shape
    depth, columns = rotation.shape
    bf16 = jnp.bfloat16
    rest = columns // CHUNKS * LEFT
    dma = pltpu.SemaphoreType.DMA
    vmem = pl.BlockSpec(memory_space=pltpu.VMEM)
    hbm = pl.BlockSpec(memory_space=pltpu.HBM)
    first, gathered, all_points = pl.pallas_call(
        gather_multiply,
        out_shape=(
            pltpu.VMEM((points, columns - rest), bf16),
            pltpu.VMEM((2, 2, 2, depth, columns), bf16),
            pltpu.VMEM((points, 4 * inner), bf16),
        ),
        in_specs=[hbm] * 2,
        out_specs=(vmem,) * 3,
        scratch_shapes=[
            dma((2, EARLY)), dma((2, EARLY)),
            dma((2, CHUNKS)), dma((2, CHUNKS)),
            dma((CHUNKS,)), dma((CHUNKS,)),
            dma((2, 3)), dma((2, 3)),
            dma((2,)),
        ],
        compiler_params=pltpu.CompilerParams(
            collective_id=0, has_side_effects=True, vmem_limit_bytes=16 * 2**20
        ),
        cost_estimate=pl.CostEstimate(
            flops=2 * points * 8 * depth * (columns - rest),
            bytes_accessed=2 * (points * inner + depth * columns),
            transcendentals=0,
        ),
        name="gather_multiply",
    )(
        pltpu.with_memory_space_constraint(orbitals, pltpu.HBM),
        pltpu.with_memory_space_constraint(rotation, pltpu.HBM),
    )
    keep = functools.partial(pltpu.with_memory_space_constraint, memory_space=pltpu.VMEM)
    return pl.pallas_call(
        write_rest,
        out_shape=pltpu.HBM((points, columns), bf16),
        in_specs=[vmem] * 3,
        out_specs=hbm,
        scratch_shapes=[pltpu.VMEM((points, rest), bf16), dma((BLOCKS + LEFT,))],
        compiler_params=pltpu.CompilerParams(vmem_limit_bytes=16 * 2**20),
        cost_estimate=pl.CostEstimate(
            flops=2 * points * 8 * depth * rest,
            bytes_accessed=2 * points * columns,
            transcendentals=0,
        ),
        name="write_rest",
    )(keep(first), keep(gathered), keep(all_points))


def with_collectives(orbitals, rotation):
    all_cols = lax.all_gather(orbitals, "band", axis=1, tiled=True)
    all_rows = lax.all_gather(rotation, "grid", axis=0, tiled=True)
    total = jnp.dot(all_cols, all_rows, preferred_element_type=jnp.float32)
    return total.astype(jnp.bfloat16)


def solution(mesh):
    specs = (P("grid", "band"), P("grid", "band"))

    def on_device(orbitals, rotation):
        square = mesh.shape["grid"] == 8 and mesh.shape["band"] == 4
        fits = (
            orbitals.shape[1] % 128 == 0
            and rotation.shape[0] % 64 == 0
            and rotation.shape[1] % (128 * CHUNKS) == 0
        )
        return (in_kernel if square and fits else with_collectives)(orbitals, rotation)

    return jax.shard_map(
        on_device, mesh=mesh, in_specs=specs, out_specs=P("grid", "band"), check_vma=False
    )
```
